512 devices in a mesh: pipe: 32 (over y_hi, z), seq: 16 (over x, y_lo, core).
Axes of the slice: x: 4, y: 8 (y_hi: 4, y_lo: 2; y = y_hi * 2 + y_lo), z: 8, core: 2. Of those that a mesh axis runs over, the one named last changes fastest.
Arguments:
- activations: bfloat16 [32, 1024, 3072], P('pipe', 'seq'), may hold values from -6 to 6
- modulation: float32 [32, 3, 3072], P('pipe'), may hold values from -3 to 3
- w_qkv: bfloat16 [32, 3072, 3, 2048], P('pipe', None, None, 'seq'), may hold values from -0.109375 to 0.109375
- w_out: bfloat16 [32, 2048, 3072], P('pipe', None, 'seq'), may hold values from -0.125 to 0.125
- stale_kv: bfloat16 [32, 2, 1536, 2048], P('pipe', None, 'seq'), may hold values from -172 to 172
- section_micro: int32 [32], P('pipe'), may hold values from 0 to 3
- patch_micro: int32 [1536], replicated, may hold values from 0 to 3, as said below
Outputs:
- handed: bfloat16 [32, 1024, 3072], P('pipe', 'seq')
The draws below stay inside these ranges and needn't reach their ends.
Inputs may be any that keep to these rules, and one draw needn't show every extreme that they name: `patch_micro`: each micro-batch index owns exactly 384 rows.
All inputs are finite; a program needn't handle non-finite values.
Results may differ from the reference program's by a relative error of at most 0.02.
The reference program's roundings to bfloat16 on the way count: a program that leaves them out, or rounds other values in their place, can miss the bound.
Values may be sent and summed in bfloat16 or wider, within the bound.
No kernel may reach another device: no remote copies, remote signals or barrier semaphores. Data moves between devices by JAX's collectives and lax.ppermute only.
A program may use at most 64 MiB of HBM per device.

```python
import jax
import jax.numpy as jnp
from jax import lax

D = 3072
H = 16
HD = 128
MICROS = 4
SECTIONS = 32
MB_TOK = 1024
KV_LEN = 1536


def draw_patch_micro(key, part):
    key = jax.random.fold_in(key, 1)
    order = jax.random.permutation(key, KV_LEN)
    return (order % MICROS).astype(jnp.int32)


def draw_stale_kv(key, part):
    key = jax.random.fold_in(key, 2)
    shape = (SECTIONS, 2, KV_LEN, H * HD)
    base = jnp.clip(jax.random.normal(key, shape, jnp.float32), -4.0, 4.0)
    return jnp.stack([base[:, 0], 6.0 * base[:, 1]], axis=1).astype(jnp.bfloat16)


def touch_ends(result, rng, low, top_value):
    longest = result.shape.index(max(result.shape))
    spots = []
    for shift in (0, 1):
        where = [jax.random.randint(jax.random.fold_in(rng, axis), (), 0, length) for axis, length in enumerate(result.shape)]
        where[longest] = (where[longest] + shift) % result.shape[longest]
        spots.append(tuple(where))
    return result.at[spots[0]].set(low).at[spots[1]].set(top_value)


def level_of(rng, shape, split, smallest, top_value):
    def one(position, parts):
        draws = jax.random.uniform(jax.random.fold_in(jax.random.fold_in(rng, 6), position), (parts,), jnp.float32, smallest / len(split), top_value / len(split))
        return jnp.repeat(jnp.exp(draws), shape[position] // parts).reshape((-1,) + (1,) * (len(shape) - position - 1))

    factor_of = one(*split[0])
    for cut in split[1:]:
        factor_of = factor_of * one(*cut)
    return factor_of


def bell_draw(stream_key, extent, spread, most, split=(), kind=jnp.bfloat16):
    drawn = jax.random.normal(stream_key, extent, jnp.float32) * spread
    if len(split) > 0:
        drawn = level_of(stream_key, extent, split, -0.22, 0.18) * drawn
    return jnp.clip(drawn, min=-most, max=most).astype(kind)


def setup_inputs(seed: int = 0) -> dict:
    splits = jax.random.split(jax.random.key(seed), 8)
    activations = bell_draw(splits[0], (SECTIONS, MB_TOK, D), 1.0, 6.0, ((0, 32), (1, 16)))
    modulation = bell_draw(splits[1], (SECTIONS, 3, D), 1.0, 3.0, ((0, 32),), jnp.float32)
    w_qkv = bell_draw(splits[2], (SECTIONS, D, 3, H * HD), D ** -0.5, 0.109375, ((0, 32), (3, 16)))
    w_out = bell_draw(splits[3], (SECTIONS, H * HD, D), (H * HD) ** -0.5, 0.125, ((0, 32), (2, 16)))
    stale_kv = draw_stale_kv(jax.random.fold_in(splits[7], 71), 0)
    section_micro = touch_ends(jax.random.randint(splits[5], (SECTIONS,), 0, MICROS), jax.random.fold_in(splits[5], 1), 0, MICROS - 1).astype(jnp.int32)
    patch_micro = draw_patch_micro(jax.random.fold_in(splits[7], 71), 0)
    return dict(activations=activations, modulation=modulation, w_qkv=w_qkv, w_out=w_out, stale_kv=stale_kv, section_micro=section_micro, patch_micro=patch_micro)


def normalize(rows, shift, scale):
    values = rows.astype(jnp.float32)
    mean = lax.optimization_barrier(jnp.mean(values, axis=-1, keepdims=True))
    centred = values - mean
    var = lax.optimization_barrier(jnp.mean(centred * centred, axis=-1, keepdims=True))
    normed = centred * lax.rsqrt(var + 1e-06)
    return (normed * (1.0 + scale) + shift).astype(jnp.bfloat16)

def attend(query, keys, values, keep_all):
    scores = jnp.dot(query, keys.T, preferred_element_type=jnp.float32) * HD ** (-0.5)
    scores = jnp.where(keep_all[None, :], scores, -jnp.inf)
    top = lax.optimization_barrier(jnp.max(scores, axis=-1, keepdims=True))
    expo = jnp.exp(scores - top)
    weights = (expo / lax.optimization_barrier(jnp.sum(expo, axis=-1, keepdims=True))).astype(jnp.bfloat16)
    return jnp.dot(weights, values, preferred_element_type=jnp.float32).astype(jnp.bfloat16)

def reference(activations, modulation, w_qkv, w_out, stale_kv, section_micro, patch_micro):

    def one_section(item):
        rows, mod, weight_in, weight_out, stale, micro = item
        hidden = normalize(rows, mod[0], mod[1])
        qkv = jnp.dot(hidden, weight_in.reshape(D, 3 * H * HD), preferred_element_type=jnp.float32)
        qkv = qkv.astype(jnp.bfloat16).reshape(MB_TOK, 3, H, HD)
        keep_all = jnp.concatenate([jnp.ones((MB_TOK,), bool), patch_micro != micro])
        query = jnp.transpose(qkv[:, 0], (1, 0, 2))
        stale_heads = jnp.transpose(stale.reshape(2, KV_LEN, H, HD), (0, 2, 1, 3))
        keys = jnp.concatenate([jnp.transpose(qkv[:, 1], (1, 0, 2)), stale_heads[0]], axis=1)
        values = jnp.concatenate([jnp.transpose(qkv[:, 2], (1, 0, 2)), stale_heads[1]], axis=1)
        heads = lax.map(lambda trio: attend(trio[0], trio[1], trio[2], keep_all), (query, keys, values))
        heads_out = jnp.transpose(heads, (1, 0, 2)).reshape(MB_TOK, H * HD)
        attn = jnp.dot(heads_out, weight_out, preferred_element_type=jnp.float32).astype(jnp.bfloat16)
        return (rows.astype(jnp.float32) + mod[2] * attn.astype(jnp.float32)).astype(jnp.bfloat16)
    results = lax.map(one_section, (activations, modulation, w_qkv, w_out, stale_kv, section_micro))
    return jnp.roll(results, 1, axis=0)
```

```python
import jax
import jax.numpy as jnp
from jax import lax
from jax.experimental import pallas as pl
from jax.experimental.pallas import tpu as pltpu
from jax.sharding import PartitionSpec as P

HD = 128
NX, NY, NC = 4, 2, 2
MIB = 1024 * 1024


def microseconds(time):
    return pl.CostEstimate(flops=int(time * 1e9), bytes_accessed=1, transcendentals=0)


X_GROUPS = [[x * NY * NC + rest for x in range(NX)] for rest in range(NY * NC)]


def seq_index(x, y, core):
    return (x % NX) * NY * NC + (y % NY) * NC + core % NC


def shift(value, dx=0, dy=0, dc=0):
    pairs = [
        (seq_index(x, y, c), seq_index(x + dx, y + dy, c + dc))
        for x in range(NX)
        for y in range(NY)
        for c in range(NC)
    ]
    return lax.ppermute(value, "seq", pairs)


def along_x(rows):
    sent = jnp.broadcast_to(rows[None], (NX, *rows.shape))
    return lax.all_to_all(sent, "seq", 0, 0, tiled=True, axis_index_groups=X_GROUPS)


def hand_on(value, dx):
    count = lax.axis_size("pipe")
    pairs = [
        (s * 16 + seq_index(x, y, c), ((s + 1) % count) * 16 + seq_index(x + dx, y, c))
        for s in range(count)
        for x in range(NX)
        for y in range(NY)
        for c in range(NC)
    ]
    return lax.ppermute(value, ("pipe", "seq"), pairs)


def following(first, *values):
    return lax.optimization_barrier((first, *values))[1:]


def whole(count):
    return [pl.BlockSpec(memory_space=pltpu.VMEM)] * count


SCALAR = pl.BlockSpec(memory_space=pltpu.SMEM)


def place(me_ref):
    me = me_ref[0]
    return me >> 2, (me >> 1) & 1, me & 1


def qkv_kernel(rows, mod, w_own, w_sib, own, sib, hidden):
    shift_row = mod[0:1, :]
    scale_row = 1.0 + mod[1:2, :]
    for i in range(NX):
        values = rows[i].astype(jnp.float32)
        mean = jnp.mean(values, axis=-1, keepdims=True)
        centred = values - mean
        var = jnp.mean(centred * centred, axis=-1, keepdims=True)
        normed = centred * lax.rsqrt(var + 1e-06)
        hidden[64 * i : 64 * i + 64, :] = (normed * scale_row + shift_row).astype(jnp.bfloat16)
    parts = [w_own.at[i] for i in range(3)] + [w_sib.at[i] for i in range(3)]
    for pair in range(3):
        weight = jnp.concatenate([parts[2 * pair][...], parts[2 * pair + 1][...]], axis=-1)
        out = jnp.dot(hidden[...], weight, preferred_element_type=jnp.float32).astype(jnp.bfloat16)
        for half in range(2):
            at = 2 * pair + half
            target = own if at < 3 else sib
            target[:, 128 * (at % 3) : 128 * (at % 3) + 128] = out[:, 128 * half : 128 * half + 128]


def project_qkv(rows, mod, w_own, w_sib):
    shape = jax.ShapeDtypeStruct((256, 3 * HD), jnp.bfloat16)
    return pl.pallas_call(
        qkv_kernel,
        out_shape=(shape, shape),
        in_specs=whole(4),
        out_specs=tuple(whole(2)),
        scratch_shapes=[pltpu.VMEM((256, 3072), jnp.bfloat16)],
        compiler_params=pltpu.CompilerParams(vmem_limit_bytes=16 * MIB),
        cost_estimate=microseconds(4.5),
    )(rows, mod, w_own, w_sib)


def attend_kernel(me_ref, micro, patch, p1, s1, p2, s2, stale, out, query, keys, values):
    x, y, c = place(me_ref)
    for i, ref in enumerate((p1, s1, p2, s2)):
        query[i] = ref[:, 0:128]
        keys[256 * i : 256 * i + 256, :] = ref[:, 128:256]
        values[256 * i : 256 * i + 256, :] = ref[:, 256:384]
    for j in range(16):
        keys[1024 + 96 * j : 1120 + 96 * j, :] = stale[j, 0]
        values[1024 + 96 * j : 1120 + 96 * j, :] = stale[j, 1]
    hide = jnp.where(patch[...] != micro[0], 0.0, -jnp.inf)
    for i, (dy, dc) in enumerate(((0, 0), (0, 1), (1, 0), (1, 1))):
        scores = lax.dot_general(
            query[i], keys[...], (((1,), (1,)), ((), ())), preferred_element_type=jnp.float32
        ) * HD ** (-0.5)
        fresh = scores[:, :1024]
        old = scores[:, 1024:] + hide
        top = jnp.maximum(
            jnp.max(fresh, axis=-1, keepdims=True), jnp.max(old, axis=-1, keepdims=True)
        )
        fresh = jnp.exp(fresh - top)
        old = jnp.exp(old - top)
        total = jnp.sum(fresh, axis=-1, keepdims=True) + jnp.sum(old, axis=-1, keepdims=True)
        part = 1.0 / total
        weights = jnp.concatenate(
            [(fresh * part).astype(jnp.bfloat16), (old * part).astype(jnp.bfloat16)], axis=-1
        )
        result = jnp.dot(weights, values[...], preferred_element_type=jnp.float32).astype(jnp.bfloat16)
        group = (y ^ dy) * 2 + (c ^ dc)
        for owner in range(NX):
            for to in range(NX):
                out[to, group, (owner - to) % NX] = result[64 * owner : 64 * owner + 64]


def attend(me, micro, patch, parts, stale):
    return pl.pallas_call(
        attend_kernel,
        out_shape=jax.ShapeDtypeStruct((NX, 4, NX, 64, HD), jnp.bfloat16),
        in_specs=[SCALAR, SCALAR] + whole(6),
        out_specs=whole(1)[0],
        scratch_shapes=[
            pltpu.VMEM((4, 256, HD), jnp.bfloat16),
            pltpu.VMEM((2560, HD), jnp.bfloat16),
            pltpu.VMEM((2560, HD), jnp.bfloat16),
        ],
        compiler_params=pltpu.CompilerParams(vmem_limit_bytes=16 * MIB),
        cost_estimate=microseconds(7),
    )(me, micro, patch, *parts, stale)


def out_kernel(me_ref, heads, w_own, w_c, w_y, w_yc, mod, held, o0, o1, o2, o3, weight):
    x, y, c = place(me_ref)
    for ref, dy, dc in ((w_own, 0, 0), (w_c, 0, 1), (w_y, 1, 0), (w_yc, 1, 1)):
        at = pl.multiple_of(((y ^ dy) * 2 + (c ^ dc)) * 192, 64)
        weight[pl.ds(at, 192), :] = ref[...]
    rows = jnp.concatenate([heads[j] for j in range(16)], axis=-1)
    attn = lax.dot_general(
        rows, weight[...], (((1,), (1,)), ((), ())), preferred_element_type=jnp.float32
    ).astype(jnp.bfloat16).astype(jnp.float32)
    columns = pl.ds(pl.multiple_of(x * 768, 768), 768)
    gate = mod[2:3, columns]
    for i, out in enumerate((o0, o1, o2, o3)):
        values = held[(x + i) & 3, :, columns].astype(jnp.float32)
        out[...] = (values + gate * attn[64 * i : 64 * i + 64, :]).astype(jnp.bfloat16)


def project_out(me, heads, weights, mod, rows):
    shape = jax.ShapeDtypeStruct((64, 768), jnp.bfloat16)
    return pl.pallas_call(
        out_kernel,
        out_shape=(shape,) * 4,
        in_specs=[SCALAR] + whole(7),
        out_specs=tuple(whole(4)),
        scratch_shapes=[pltpu.VMEM((768, 2048), jnp.bfloat16)],
        compiler_params=pltpu.CompilerParams(vmem_limit_bytes=16 * MIB),
        cost_estimate=microseconds(1.5),
    )(me, heads, *weights, mod, rows)


def join_kernel(me_ref, p0, p1, p2, p3, out):
    x, _, _ = place(me_ref)
    for i, ref in enumerate((p0, p1, p2, p3)):
        out[:, pl.ds(pl.multiple_of(((x + NX - i) & 3) * 768, 768), 768)] = ref[...]


def join(me, pieces):
    return pl.pallas_call(
        join_kernel,
        out_shape=jax.ShapeDtypeStruct((64, 3072), jnp.bfloat16),
        in_specs=[SCALAR] + whole(4),
        out_specs=whole(1)[0],
        cost_estimate=microseconds(1.5),
    )(me, *pieces)


def on_device(activations, modulation, w_qkv, w_out, stale_kv, section_micro, patch_micro):
    rows = activations[0]
    mod = modulation[0]
    me = lax.axis_index("seq").astype(jnp.int32).reshape(1)
    w_own = jnp.transpose(w_qkv[0], (1, 0, 2))
    out_own = jnp.transpose(w_out[0], (1, 0))

    across = shift(rows, dy=1)
    near = along_x(rows)
    w_sib = shift(w_own, dc=1)
    there = along_x(across)
    (out_late,) = following(across, out_own)
    out_y = shift(out_late, dy=1)

    own_1, theirs = project_qkv(near, mod, w_own, w_sib)
    sib_1 = shift(theirs, dc=1)
    stale, out_late = following(own_1, stale_kv[0], out_own)
    out_c = shift(out_late, dc=1)
    stale = stale.reshape(2, 96, 16, HD).transpose(2, 0, 1, 3)
    stale = lax.all_to_all(stale, "seq", 0, 0, tiled=True)
    own_2, theirs = project_qkv(there, mod, w_own, w_sib)
    sib_2 = shift(theirs, dc=1)
    out_yc = shift(out_y, dc=1)
    own_2, out_yc = lax.optimization_barrier((own_2, out_yc))

    heads = attend(me, section_micro, patch_micro.reshape(1, -1), (own_1, sib_1, own_2, sib_2), stale)
    heads = lax.all_to_all(heads.reshape(16, 256, HD), "seq", 0, 0, tiled=True)
    pieces = project_out(me, heads, (out_own, out_c, out_y, out_yc), mod, near)
    pieces = [hand_on(piece, dx) for dx, piece in enumerate(pieces)]
    return join(me, pieces)[None]


def solution(mesh):
    return jax.shard_map(
        on_device,
        mesh=mesh,
        in_specs=(
            P("pipe", "seq", None),
            P("pipe", None, None),
            P("pipe", None, None, "seq"),
            P("pipe", None, "seq"),
            P("pipe", None, "seq", None),
            P("pipe"),
            P(),
        ),
        out_specs=P("pipe", "seq", None),
        check_vma=False,
    )
```

```python
import math

import jax
import jax.numpy as jnp
from jax import lax
from jax.experimental import pallas as pl
from jax.experimental.pallas import tpu as pltpu
from jax.sharding import PartitionSpec as P

HD = 128
NX, NY, NC = 4, 2, 2
MIB = 1024 * 1024
SCALAR = pl.BlockSpec(memory_space=pltpu.SMEM)
FAR = pl.BlockSpec(memory_space=pltpu.HBM)
NEAR = pl.BlockSpec(memory_space=pltpu.VMEM)


def seq_index(x, y, core):
    return (x % NX) * NY * NC + (y % NY) * NC + core % NC


LANES = [[seq_index(x, y, c) for x in range(NX) for y in range(NY)] for c in range(NC)]


def shift(value, dx=0, dy=0, dc=0):
    pairs = [
        (seq_index(x, y, c), seq_index(x + dx, y + dy, c + dc))
        for x in range(NX)
        for y in range(NY)
        for c in range(NC)
    ]
    return lax.ppermute(value, "seq", pairs)


def hand_on(value, dx):
    count = lax.axis_size("pipe")
    pairs = [
        (s * 16 + seq_index(x, y, c), ((s + 1) % count) * 16 + seq_index(x + dx, y, c))
        for s in range(count)
        for x in range(NX)
        for y in range(NY)
        for c in range(NC)
    ]
    return lax.ppermute(value, ("pipe", "seq"), pairs)


def following(first, *values):
    return lax.optimization_barrier((first, *values))[1:]


def cost(microseconds):
    return pl.CostEstimate(flops=int(microseconds * 1e9), bytes_accessed=1, transcendentals=0)


def params(mib):
    return pltpu.CompilerParams(vmem_limit_bytes=mib * MIB)


def place(me_ref):
    me = me_ref[0]
    return me >> 2, (me >> 1) & 1, me & 1


def pack_kernel(rows, stale, out, held, old, load_sems, row_sems, stale_sems):
    loads = [
        pltpu.make_async_copy(rows, held, load_sems.at[0]),
        pltpu.make_async_copy(stale, old, load_sems.at[1]),
    ]
    for load in loads:
        load.start()
    copies = []
    loads[0].wait()
    for to in range(8):
        copies.append(pltpu.make_async_copy(held, out.at[to, :, 0:3072], row_sems.at[to]))
        copies[-1].start()
    loads[1].wait()
    for to in range(8):
        for t in range(3):
            copies.append(
                pltpu.make_async_copy(
                    old.at[64 * t : 64 * t + 64, 256 * to : 256 * to + 256],
                    out.at[to, :, 3072 + 256 * t : 3328 + 256 * t],
                    stale_sems.at[3 * to + t],
                )
            )
            copies[-1].start()
    for copy in copies:
        copy.wait()


def pack(rows, stale):
    return pl.pallas_call(
        pack_kernel,
        out_shape=jax.ShapeDtypeStruct((8, 64, 3840), jnp.bfloat16),
        in_specs=[FAR, FAR],
        out_specs=FAR,
        scratch_shapes=[
            pltpu.VMEM((64, 3072), jnp.bfloat16),
            pltpu.VMEM((192, 2048), jnp.bfloat16),
            pltpu.SemaphoreType.DMA((2,)),
            pltpu.SemaphoreType.DMA((8,)),
            pltpu.SemaphoreType.DMA((24,)),
        ],
        compiler_params=params(60),
        cost_estimate=cost(3),
    )(rows, stale)


def weights_kernel(w_own, w_sib, weight, sems):
    copies = []
    for i, ref in enumerate((w_sib, w_own)):
        copies.append(pltpu.make_async_copy(ref, weight.at[pl.ds(3 * i, 3)], sems.at[i]))
        copies[-1].start()
    for copy in copies:
        copy.wait()


def collect_weights(w_own, w_sib):
    return pl.pallas_call(
        weights_kernel,
        out_shape=jax.ShapeDtypeStruct((6, 3072, HD), jnp.bfloat16),
        in_specs=[FAR, FAR],
        out_specs=NEAR,
        scratch_shapes=[pltpu.SemaphoreType.DMA((2,))],
        compiler_params=params(16),
        cost_estimate=cost(0.01),
    )(w_own, w_sib)


def qkv_kernel(me_ref, gathered, mod, weight, own, own_old, sib, sib_old, hidden):
    _, _, c = place(me_ref)
    shift_row = mod[0:1, :]
    scale_row = 1.0 + mod[1:2, :]
    for out, head in ((sib_old, 1 - c), (own_old, c)):
        for t in range(3):
            at = pl.multiple_of(3072 + 256 * t + 128 * head, 128)
            out[:, :, 128 * t : 128 * t + 128] = gathered[:, :, pl.ds(at, 128)]
    for half in range(2):
        for i in range(4 * half, 4 * half + 4):
            values = gathered[i, :, 0:3072].astype(jnp.float32)
            mean = jnp.mean(values, axis=-1, keepdims=True)
            centred = values - mean
            var = jnp.mean(centred * centred, axis=-1, keepdims=True)
            normed = centred * lax.rsqrt(var + 1e-06)
            hidden[64 * i : 64 * i + 64, :] = (normed * scale_row + shift_row).astype(jnp.bfloat16)
        for pair in range(3):
            both = jnp.concatenate([weight[2 * pair], weight[2 * pair + 1]], axis=-1)
            result = jnp.dot(
                hidden[256 * half : 256 * half + 256, :], both, preferred_element_type=jnp.float32
            ).astype(jnp.bfloat16)
            for n in range(2):
                at = 2 * pair + n
                target = sib if at < 3 else own
                target[4 * half : 4 * half + 4, :, 128 * (at % 3) : 128 * (at % 3) + 128] = result[
                    :, 128 * n : 128 * n + 128
                ].reshape(4, 64, HD)


def project_qkv(me, gathered, mod, weight):
    shape = jax.ShapeDtypeStruct((8, 64, 3 * HD), jnp.bfloat16)
    return pl.pallas_call(
        qkv_kernel,
        out_shape=(shape,) * 4,
        in_specs=[SCALAR, NEAR, NEAR, NEAR],
        out_specs=(NEAR,) * 4,
        scratch_shapes=[pltpu.VMEM((512, 3072), jnp.bfloat16)],
        compiler_params=params(24),
        cost_estimate=cost(0.01),
    )(me, gathered, mod, weight)


def attend_kernel(me_ref, hide, own, own_old, sib, sib_old, out, query, keys, values, staged, out_sems):
    _, _, c = place(me_ref)
    for i, (new, old) in enumerate(((own, own_old), (sib, sib_old))):
        fresh = slice(512 * i, 512 * i + 512)
        query[fresh, :] = new[:, :, 0:128].reshape(512, HD)
        keys[fresh, :] = new[:, :, 128:256].reshape(512, HD)
        values[fresh, 0:128] = new[:, :, 256:384].reshape(512, HD)
        for k in range(8):
            at = 1024 + 96 * (8 * i + k)
            keys[at : at + 64, :] = old[k, :, 0:128]
            keys[at + 64 : at + 96, :] = old[k, 0:32, 128:256]
            values[at : at + 32, 0:128] = old[k, 32:64, 128:256]
            values[at + 32 : at + 96, 0:128] = old[k, :, 256:384]
    values[:, 128:256] = jnp.ones((2560, 128), jnp.bfloat16)
    scale = HD ** (-0.5) * math.log2(math.e)
    for i in range(8):
        scores = lax.dot_general(
            query[128 * i : 128 * i + 128, :],
            keys[...],
            (((1,), (1,)), ((), ())),
            preferred_element_type=jnp.float32,
        )
        fresh = scores[:, :1024]
        old = scores[:, 1024:] + hide[...]
        top = jnp.maximum(
            jnp.max(fresh, axis=-1, keepdims=True), jnp.max(old, axis=-1, keepdims=True)
        )
        weights = jnp.concatenate(
            [
                jnp.exp2((fresh - top) * scale).astype(jnp.bfloat16),
                jnp.exp2((old - top) * scale).astype(jnp.bfloat16),
            ],
            axis=-1,
        )
        summed = jnp.dot(weights, values[...], preferred_element_type=jnp.float32)
        result = (summed[:, :128] * (1.0 / summed[:, 128:])).astype(jnp.bfloat16)
        for n in range(2):
            dc, owner, y = i // 4, i % 4, n
            for to in range(NX):
                staged[to, y * 2 + (c ^ dc), (owner - to) % NX] = result[64 * n : 64 * n + 64]
    stores = []
    for to in range(NX):
        stores.append(pltpu.make_async_copy(staged.at[to], out.at[to], out_sems.at[to]))
        stores[-1].start()
    for store in stores:
        store.wait()


def attend(me, hide, own, own_old, sib, sib_old):
    return pl.pallas_call(
        attend_kernel,
        out_shape=jax.ShapeDtypeStruct((NX, 4, NX, 64, HD), jnp.bfloat16),
        in_specs=[SCALAR] + [NEAR] * 5,
        out_specs=FAR,
        scratch_shapes=[
            pltpu.VMEM((1024, HD), jnp.bfloat16),
            pltpu.VMEM((2560, HD), jnp.bfloat16),
            pltpu.VMEM((2560, 2 * HD), jnp.bfloat16),
            pltpu.VMEM((NX, 4, NX, 64, HD), jnp.bfloat16),
            pltpu.SemaphoreType.DMA((NX,)),
        ],
        compiler_params=params(32),
        cost_estimate=cost(0.01),
    )(me, hide, own, own_old, sib, sib_old)


def out_kernel(me_ref, heads, w_own, w_c, w_y, w_yc, mod, gathered, o0, o1, o2, o3, weight, held, w_sems, sems):
    x, y, c = place(me_ref)
    parts = []
    for i, (ref, dy, dc) in enumerate(((w_own, 0, 0), (w_c, 0, 1), (w_y, 1, 0), (w_yc, 1, 1))):
        at = pl.multiple_of(((y ^ dy) * 2 + (c ^ dc)) * 192, 64)
        parts.append(pltpu.make_async_copy(ref, weight.at[pl.ds(at, 192), :], w_sems.at[i]))
        parts[-1].start()
    columns = pl.ds(pl.multiple_of(x * 768, 768), 768)
    loads = [
        pltpu.make_async_copy(
            gathered.at[((x + i) & 3) * 2 + y, :, columns], held.at[i], sems.at[i]
        )
        for i in range(4)
    ]
    for load in loads:
        load.start()
    rows = jnp.concatenate([heads[j] for j in range(16)], axis=-1)
    for part in parts:
        part.wait()
    attn = lax.dot_general(
        rows, weight[...], (((1,), (1,)), ((), ())), preferred_element_type=jnp.float32
    ).astype(jnp.bfloat16).astype(jnp.float32)
    gate = mod[2:3, columns]
    for i, out in enumerate((o0, o1, o2, o3)):
        loads[i].wait()
        values = held[i].astype(jnp.float32)
        out[...] = (values + gate * attn[64 * i : 64 * i + 64, :]).astype(jnp.bfloat16)


def project_out(me, heads, weights, mod, gathered):
    shape = jax.ShapeDtypeStruct((64, 768), jnp.bfloat16)
    return pl.pallas_call(
        out_kernel,
        out_shape=(shape,) * 4,
        in_specs=[SCALAR, NEAR] + [FAR] * 4 + [NEAR, FAR],
        out_specs=(NEAR,) * 4,
        scratch_shapes=[
            pltpu.VMEM((768, 2048), jnp.bfloat16),
            pltpu.VMEM((4, 64, 768), jnp.bfloat16),
            pltpu.SemaphoreType.DMA((4,)),
            pltpu.SemaphoreType.DMA((4,)),
        ],
        compiler_params=params(32),
        cost_estimate=cost(2),
    )(me, heads, *weights, mod, gathered)


def join_kernel(me_ref, p0, p1, p2, p3, out, sems):
    x, _, _ = place(me_ref)
    copies = []
    for i, ref in enumerate((p0, p1, p2, p3)):
        columns = pl.ds(pl.multiple_of(((x + NX - i) & 3) * 768, 768), 768)
        copies.append(pltpu.make_async_copy(ref, out.at[:, columns], sems.at[i]))
        copies[-1].start()
    for copy in copies:
        copy.wait()


def join(me, pieces):
    return pl.pallas_call(
        join_kernel,
        out_shape=jax.ShapeDtypeStruct((64, 3072), jnp.bfloat16),
        in_specs=[SCALAR] + [NEAR] * 4,
        out_specs=FAR,
        scratch_shapes=[pltpu.SemaphoreType.DMA((4,))],
        compiler_params=params(32),
        cost_estimate=cost(0.01),
    )(me, *pieces)


def on_device(activations, modulation, w_qkv, w_out, stale_kv, section_micro, patch_micro):
    rows = activations[0]
    mod = modulation[0]
    index = lax.axis_index("seq").astype(jnp.int32)
    me = index.reshape(1)
    w_own = jnp.transpose(w_qkv[0], (1, 0, 2))
    out_own = jnp.transpose(w_out[0], (1, 0))
    owners = patch_micro.reshape(8, 2, 96).transpose(1, 0, 2)
    owners = jnp.where(index % 2 == 0, owners, owners[::-1]).reshape(1, -1)
    hide = jnp.where(owners != section_micro[0], 0.0, -jnp.inf).astype(jnp.float32)

    sent = pack(rows, stale_kv[0].reshape(192, 2048))
    gathered = lax.all_to_all(sent, "seq", 0, 0, tiled=True, axis_index_groups=LANES)
    w_sib = shift(w_own, dc=1)
    out_c = shift(out_own, dc=1)
    (out_late,) = following(gathered, out_own)
    out_y = shift(out_late, dy=1)
    out_yc = shift(out_y, dc=1)
    own, own_old, sib, sib_old = project_qkv(me, gathered, mod, collect_weights(w_own, w_sib))
    sib = shift(sib, dc=1)
    sib_old = shift(sib_old, dc=1)
    heads = attend(me, hide, own, own_old, sib, sib_old)
    (heads,) = following(out_y, heads)
    heads = lax.all_to_all(heads.reshape(16, 256, HD), "seq", 0, 0, tiled=True)
    pieces = project_out(me, heads, (out_own, out_c, out_y, out_yc), mod, gathered)
    pieces = [hand_on(piece, dx) for dx, piece in enumerate(pieces)]
    return join(me, pieces)[None]


def solution(mesh):
    return jax.shard_map(
        on_device,
        mesh=mesh,
        in_specs=(
            P("pipe", "seq", None),
            P("pipe", None, None),
            P("pipe", None, None, "seq"),
            P("pipe", None, "seq"),
            P("pipe", None, "seq", None),
            P("pipe"),
            P(),
        ),
        out_specs=P("pipe", "seq", None),
        check_vma=False,
    )
```

```python
import math

import jax
import jax.numpy as jnp
from jax import lax
from jax.experimental import pallas as pl
from jax.experimental.pallas import tpu as pltpu
from jax.sharding import PartitionSpec as P

HD = 128
NX, NY, NC = 4, 2, 2
MIB = 1024 * 1024
SCALAR = pl.BlockSpec(memory_space=pltpu.SMEM)
FAR = pl.BlockSpec(memory_space=pltpu.HBM)
NEAR = pl.BlockSpec(memory_space=pltpu.VMEM)


def seq_index(x, y, core):
    return (x % NX) * NY * NC + (y % NY) * NC + core % NC


LANES = [[seq_index(x, y, c) for x in range(NX) for y in range(NY)] for c in range(NC)]


def shift(value, dx=0, dy=0, dc=0):
    pairs = [
        (seq_index(x, y, c), seq_index(x + dx, y + dy, c + dc))
        for x in range(NX)
        for y in range(NY)
        for c in range(NC)
    ]
    return lax.ppermute(value, "seq", pairs)


def hand_on(value, dx):
    count = lax.axis_size("pipe")
    pairs = [
        (s * 16 + seq_index(x, y, c), ((s + 1) % count) * 16 + seq_index(x + dx, y, c))
        for s in range(count)
        for x in range(NX)
        for y in range(NY)
        for c in range(NC)
    ]
    return lax.ppermute(value, ("pipe", "seq"), pairs)


def following(first, *values):
    return lax.optimization_barrier((first, *values))[1:]


def cost(microseconds):
    return pl.CostEstimate(flops=int(microseconds * 1e9), bytes_accessed=1, transcendentals=0)


def params(mib):
    return pltpu.CompilerParams(vmem_limit_bytes=mib * MIB)


def place(me_ref):
    me = me_ref[0]
    return me >> 2, (me >> 1) & 1, me & 1


def pack_kernel(rows, stale, out, held, old, load_sems, row_sems, stale_sems):
    loads = [
        pltpu.make_async_copy(rows, held, load_sems.at[0]),
        pltpu.make_async_copy(stale, old, load_sems.at[1]),
    ]
    for load in loads:
        load.start()
    copies = []
    loads[0].wait()
    for to in range(8):
        copies.append(pltpu.make_async_copy(held, out.at[to, :, 0:3072], row_sems.at[to]))
        copies[-1].start()
    loads[1].wait()
    for to in range(8):
        for t in range(3):
            copies.append(
                pltpu.make_async_copy(
                    old.at[64 * t : 64 * t + 64, 256 * to : 256 * to + 256],
                    out.at[to, :, 3072 + 256 * t : 3328 + 256 * t],
                    stale_sems.at[3 * to + t],
                )
            )
            copies[-1].start()
    for copy in copies:
        copy.wait()


def pack(rows, stale):
    return pl.pallas_call(
        pack_kernel,
        out_shape=jax.ShapeDtypeStruct((8, 64, 3840), jnp.bfloat16),
        in_specs=[FAR, FAR],
        out_specs=FAR,
        scratch_shapes=[
            pltpu.VMEM((64, 3072), jnp.bfloat16),
            pltpu.VMEM((192, 2048), jnp.bfloat16),
            pltpu.SemaphoreType.DMA((2,)),
            pltpu.SemaphoreType.DMA((8,)),
            pltpu.SemaphoreType.DMA((24,)),
        ],
        compiler_params=params(60),
        cost_estimate=cost(3),
    )(rows, stale)


def weights_kernel(w_own, w_sib, weight, sems):
    copies = []
    for i, ref in enumerate((w_sib, w_own)):
        copies.append(pltpu.make_async_copy(ref, weight.at[pl.ds(3 * i, 3)], sems.at[i]))
        copies[-1].start()
    for copy in copies:
        copy.wait()


def collect_weights(w_own, w_sib):
    return pl.pallas_call(
        weights_kernel,
        out_shape=jax.ShapeDtypeStruct((6, 3072, HD), jnp.bfloat16),
        in_specs=[FAR, FAR],
        out_specs=NEAR,
        scratch_shapes=[pltpu.SemaphoreType.DMA((2,))],
        compiler_params=params(16),
        cost_estimate=cost(0.01),
    )(w_own, w_sib)


def qkv_kernel(me_ref, gathered, mod, weight, own, own_old, sib, sib_old, hidden):
    _, _, c = place(me_ref)
    shift_row = mod[0:1, :]
    scale_row = 1.0 + mod[1:2, :]
    for out, head in ((sib_old, 1 - c), (own_old, c)):
        for t in range(3):
            at = pl.multiple_of(3072 + 256 * t + 128 * head, 128)
            out[:, :, 128 * t : 128 * t + 128] = gathered[:, :, pl.ds(at, 128)]
    for half in range(2):
        for i in range(4 * half, 4 * half + 4):
            values = gathered[i, :, 0:3072].astype(jnp.float32)
            mean = jnp.mean(values, axis=-1, keepdims=True)
            centred = values - mean
            var = jnp.mean(centred * centred, axis=-1, keepdims=True)
            normed = centred * lax.rsqrt(var + 1e-06)
            hidden[64 * i : 64 * i + 64, :] = (normed * scale_row + shift_row).astype(jnp.bfloat16)
        for pair in range(3):
            both = jnp.concatenate([weight[2 * pair], weight[2 * pair + 1]], axis=-1)
            result = jnp.dot(
                hidden[256 * half : 256 * half + 256, :], both, preferred_element_type=jnp.float32
            ).astype(jnp.bfloat16)
            for n in range(2):
                at = 2 * pair + n
                target = sib if at < 3 else own
                target[4 * half : 4 * half + 4, :, 128 * (at % 3) : 128 * (at % 3) + 128] = result[
                    :, 128 * n : 128 * n + 128
                ].reshape(4, 64, HD)


def project_qkv(me, gathered, mod, weight):
    shape = jax.ShapeDtypeStruct((8, 64, 3 * HD), jnp.bfloat16)
    return pl.pallas_call(
        qkv_kernel,
        out_shape=(shape,) * 4,
        in_specs=[SCALAR, NEAR, NEAR, NEAR],
        out_specs=(NEAR,) * 4,
        scratch_shapes=[pltpu.VMEM((512, 3072), jnp.bfloat16)],
        compiler_params=params(24),
        cost_estimate=cost(0.01),
    )(me, gathered, mod, weight)


def attend_kernel(me_ref, hide, own, own_old, sib, sib_old, out, query, keys, values, staged, out_sems):
    _, _, c = place(me_ref)
    for i, (new, old) in enumerate(((own, own_old), (sib, sib_old))):
        fresh = slice(512 * i, 512 * i + 512)
        query[fresh, :] = new[:, :, 0:128].reshape(512, HD)
        keys[fresh, :] = new[:, :, 128:256].reshape(512, HD)
        values[fresh, 0:128] = new[:, :, 256:384].reshape(512, HD)
        for k in range(8):
            at = 1024 + 96 * (8 * i + k)
            keys[at : at + 64, :] = old[k, :, 0:128]
            keys[at + 64 : at + 96, :] = old[k, 0:32, 128:256]
            values[at : at + 32, 0:128] = old[k, 32:64, 128:256]
            values[at + 32 : at + 96, 0:128] = old[k, :, 256:384]
    values[:, 128:256] = jnp.ones((2560, 128), jnp.bfloat16)
    scale = HD ** (-0.5) * math.log2(math.e)
    stores = []
    for i in range(8):
        scores = lax.dot_general(
            query[128 * i : 128 * i + 128, :],
            keys[...],
            (((1,), (1,)), ((), ())),
            preferred_element_type=jnp.float32,
        )
        fresh = scores[:, :1024]
        old = scores[:, 1024:] + hide[...]
        top = jnp.maximum(
            jnp.max(fresh, axis=-1, keepdims=True), jnp.max(old, axis=-1, keepdims=True)
        )
        weights = jnp.concatenate(
            [
                jnp.exp2((fresh - top) * scale).astype(jnp.bfloat16),
                jnp.exp2((old - top) * scale).astype(jnp.bfloat16),
            ],
            axis=-1,
        )
        summed = jnp.dot(weights, values[...], preferred_element_type=jnp.float32)
        result = (summed[:, :128] * (1.0 / summed[:, 128:])).astype(jnp.bfloat16)
        for n in range(2):
            dc, owner, y = i // 4, i % 4, n
            for to in range(NX):
                staged[to, y * 2 + (c ^ dc), (owner - to) % NX] = result[64 * n : 64 * n + 64]
        if owner == NX - 1:
            for y in range(NY):
                group = y * 2 + (c ^ dc)
                stores.append(
                    pltpu.make_async_copy(staged.at[:, group], out.at[:, group], out_sems.at[2 * dc + y])
                )
                stores[-1].start()
    for store in stores:
        store.wait()


def attend(me, hide, own, own_old, sib, sib_old):
    return pl.pallas_call(
        attend_kernel,
        out_shape=jax.ShapeDtypeStruct((NX, 4, NX, 64, HD), jnp.bfloat16),
        in_specs=[SCALAR] + [NEAR] * 5,
        out_specs=FAR,
        scratch_shapes=[
            pltpu.VMEM((1024, HD), jnp.bfloat16),
            pltpu.VMEM((2560, HD), jnp.bfloat16),
            pltpu.VMEM((2560, 2 * HD), jnp.bfloat16),
            pltpu.VMEM((NX, 4, NX, 64, HD), jnp.bfloat16),
            pltpu.SemaphoreType.DMA((NX,)),
        ],
        compiler_params=params(32),
        cost_estimate=cost(0.01),
    )(me, hide, own, own_old, sib, sib_old)


def collect_kernel(me_ref, w_own, w_c, w_y, w_yc, weight, sems):
    x, y, c = place(me_ref)
    copies = []
    for i, (ref, dy, dc) in enumerate(((w_own, 0, 0), (w_c, 0, 1), (w_y, 1, 0), (w_yc, 1, 1))):
        at = pl.multiple_of(((y ^ dy) * 2 + (c ^ dc)) * 192, 64)
        copies.append(pltpu.make_async_copy(ref, weight.at[pl.ds(at, 192), :], sems.at[i]))
        copies[-1].start()
    for copy in copies:
        copy.wait()


def collect(me, weights):
    return pl.pallas_call(
        collect_kernel,
        out_shape=jax.ShapeDtypeStruct((768, 2048), jnp.bfloat16),
        in_specs=[SCALAR] + [FAR] * 4,
        out_specs=NEAR,
        scratch_shapes=[pltpu.SemaphoreType.DMA((4,))],
        compiler_params=params(4),
        cost_estimate=cost(0.01),
    )(me, *weights)


def out_kernel(me_ref, heads, weight, mod, gathered, o0, o1, o2, o3, held, rows, sems, row_sems):
    x, y, _ = place(me_ref)
    columns = pl.ds(pl.multiple_of(x * 768, 768), 768)
    loads = [
        pltpu.make_async_copy(
            gathered.at[((x + i) & 3) * 2 + y, :, columns], held.at[i], sems.at[i]
        )
        for i in range(4)
    ]
    parts = [
        pltpu.make_async_copy(heads.at[4 * i : 4 * i + 4], rows.at[4 * i : 4 * i + 4], row_sems.at[i])
        for i in range(4)
    ]
    for load in parts + loads:
        load.start()
    attn = jnp.zeros((256, 768), jnp.float32)
    for i in range(4):
        parts[i].wait()
        attn += lax.dot_general(
            jnp.concatenate([rows[j] for j in range(4 * i, 4 * i + 4)], axis=-1),
            weight[:, 512 * i : 512 * i + 512],
            (((1,), (1,)), ((), ())),
            preferred_element_type=jnp.float32,
        )
    attn = attn.astype(jnp.bfloat16).astype(jnp.float32)
    gate = mod[2:3, columns]
    for i, out in enumerate((o0, o1, o2, o3)):
        loads[i].wait()
        values = held[i].astype(jnp.float32)
        out[...] = (values + gate * attn[64 * i : 64 * i + 64, :]).astype(jnp.bfloat16)


def project_out(me, heads, weight, mod, gathered):
    shape = jax.ShapeDtypeStruct((64, 768), jnp.bfloat16)
    return pl.pallas_call(
        out_kernel,
        out_shape=(shape,) * 4,
        in_specs=[SCALAR, FAR, NEAR, NEAR, FAR],
        out_specs=(NEAR,) * 4,
        scratch_shapes=[
            pltpu.VMEM((4, 64, 768), jnp.bfloat16),
            pltpu.VMEM((16, 256, HD), jnp.bfloat16),
            pltpu.SemaphoreType.DMA((4,)),
            pltpu.SemaphoreType.DMA((4,)),
        ],
        compiler_params=params(16),
        cost_estimate=cost(2),
    )(me, heads, weight, mod, gathered)


def join_kernel(me_ref, p0, p1, p2, p3, out, sems):
    x, _, _ = place(me_ref)
    copies = []
    for i, ref in enumerate((p0, p1, p2, p3)):
        columns = pl.ds(pl.multiple_of(((x + NX - i) & 3) * 768, 768), 768)
        copies.append(pltpu.make_async_copy(ref, out.at[:, columns], sems.at[i]))
        copies[-1].start()
    for copy in copies:
        copy.wait()


def join(me, pieces):
    return pl.pallas_call(
        join_kernel,
        out_shape=jax.ShapeDtypeStruct((64, 3072), jnp.bfloat16),
        in_specs=[SCALAR] + [NEAR] * 4,
        out_specs=FAR,
        scratch_shapes=[pltpu.SemaphoreType.DMA((4,))],
        compiler_params=params(32),
        cost_estimate=cost(0.01),
    )(me, *pieces)


def on_device(activations, modulation, w_qkv, w_out, stale_kv, section_micro, patch_micro):
    rows = activations[0]
    mod = modulation[0]
    index = lax.axis_index("seq").astype(jnp.int32)
    me = index.reshape(1)
    w_own = jnp.transpose(w_qkv[0], (1, 0, 2))
    out_own = jnp.transpose(w_out[0], (1, 0))
    owners = patch_micro.reshape(8, 2, 96).transpose(1, 0, 2)
    owners = jnp.where(index % 2 == 0, owners, owners[::-1]).reshape(1, -1)
    hide = jnp.where(owners != section_micro[0], 0.0, -jnp.inf).astype(jnp.float32)

    sent = pack(rows, stale_kv[0].reshape(192, 2048))
    gathered = lax.all_to_all(sent, "seq", 0, 0, tiled=True, axis_index_groups=LANES)
    w_sib = shift(w_own, dc=1)
    out_c = shift(out_own, dc=1)
    (out_late,) = following(gathered, out_own)
    out_y = shift(out_late, dy=1)
    out_yc = shift(out_y, dc=1)
    own, own_old, sib, sib_old = project_qkv(me, gathered, mod, collect_weights(w_own, w_sib))
    sib = shift(sib, dc=1)
    sib_old = shift(sib_old, dc=1)
    heads = attend(me, hide, own, own_old, sib, sib_old)
    (heads,) = following(out_y, heads)
    heads = lax.all_to_all(heads.reshape(16, 256, HD), "seq", 0, 0, tiled=True)
    pieces = project_out(me, heads, collect(me, (out_own, out_c, out_y, out_yc)), mod, gathered)
    arrived = {dx: hand_on(pieces[dx], dx) for dx in (2, 1, 3, 0)}
    return join(me, [arrived[dx] for dx in range(NX)])[None]


def solution(mesh):
    return jax.shard_map(
        on_device,
        mesh=mesh,
        in_specs=(
            P("pipe", "seq", None),
            P("pipe", None, None),
            P("pipe", None, None, "seq"),
            P("pipe", None, "seq"),
            P("pipe", None, "seq", None),
            P("pipe"),
            P(),
        ),
        out_specs=P("pipe", "seq", None),
        check_vma=False,
    )
```

```python
import math

import jax
import jax.numpy as jnp
from jax import lax
from jax.experimental import pallas as pl
from jax.experimental.pallas import tpu as pltpu
from jax.sharding import PartitionSpec as P

HD = 128
NX, NY, NC = 4, 2, 2
MIB = 1024 * 1024
SCALAR = pl.BlockSpec(memory_space=pltpu.SMEM)
FAR = pl.BlockSpec(memory_space=pltpu.HBM)
NEAR = pl.BlockSpec(memory_space=pltpu.VMEM)


def seq_index(x, y, core):
    return (x % NX) * NY * NC + (y % NY) * NC + core % NC


LANES = [[seq_index(x, y, c) for x in range(NX) for y in range(NY)] for c in range(NC)]


def shift(value, dx=0, dy=0, dc=0):
    pairs = [
        (seq_index(x, y, c), seq_index(x + dx, y + dy, c + dc))
        for x in range(NX)
        for y in range(NY)
        for c in range(NC)
    ]
    return lax.ppermute(value, "seq", pairs)


def hand_on(value, dx):
    count = lax.axis_size("pipe")
    pairs = [
        (s * 16 + seq_index(x, y, c), ((s + 1) % count) * 16 + seq_index(x + dx, y, c))
        for s in range(count)
        for x in range(NX)
        for y in range(NY)
        for c in range(NC)
    ]
    return lax.ppermute(value, ("pipe", "seq"), pairs)


def following(first, *values):
    return lax.optimization_barrier((first, *values))[1:]


def cost(microseconds):
    return pl.CostEstimate(flops=int(microseconds * 1e9), bytes_accessed=1, transcendentals=0)


def params(mib):
    return pltpu.CompilerParams(vmem_limit_bytes=mib * MIB)


def place(me_ref):
    me = me_ref[0]
    return me >> 2, (me >> 1) & 1, me & 1


def pack_kernel(rows, stale, out, held, old, load_sems, row_sems, stale_sems):
    loads = [
        pltpu.make_async_copy(rows, held, load_sems.at[0]),
        pltpu.make_async_copy(stale, old, load_sems.at[1]),
    ]
    for load in loads:
        load.start()
    copies = []
    loads[0].wait()
    for to in range(8):
        copies.append(pltpu.make_async_copy(held, out.at[to, :, 0:3072], row_sems.at[to]))
        copies[-1].start()
    loads[1].wait()
    for to in range(8):
        for t in range(3):
            copies.append(
                pltpu.make_async_copy(
                    old.at[64 * t : 64 * t + 64, 256 * to : 256 * to + 256],
                    out.at[to, :, 3072 + 256 * t : 3328 + 256 * t],
                    stale_sems.at[3 * to + t],
                )
            )
            copies[-1].start()
    for copy in copies:
        copy.wait()


def pack(rows, stale):
    return pl.pallas_call(
        pack_kernel,
        out_shape=jax.ShapeDtypeStruct((8, 64, 3840), jnp.bfloat16),
        in_specs=[FAR, FAR],
        out_specs=FAR,
        scratch_shapes=[
            pltpu.VMEM((64, 3072), jnp.bfloat16),
            pltpu.VMEM((192, 2048), jnp.bfloat16),
            pltpu.SemaphoreType.DMA((2,)),
            pltpu.SemaphoreType.DMA((8,)),
            pltpu.SemaphoreType.DMA((24,)),
        ],
        compiler_params=params(60),
        cost_estimate=cost(3),
    )(rows, stale)


def weights_kernel(w_own, w_sib, weight, sems):
    copies = []
    for i, ref in enumerate((w_sib, w_own)):
        copies.append(pltpu.make_async_copy(ref, weight.at[pl.ds(3 * i, 3)], sems.at[i]))
        copies[-1].start()
    for copy in copies:
        copy.wait()


def collect_weights(w_own, w_sib):
    return pl.pallas_call(
        weights_kernel,
        out_shape=jax.ShapeDtypeStruct((6, 3072, HD), jnp.bfloat16),
        in_specs=[FAR, FAR],
        out_specs=NEAR,
        scratch_shapes=[pltpu.SemaphoreType.DMA((2,))],
        compiler_params=params(16),
        cost_estimate=cost(0.01),
    )(w_own, w_sib)


def qkv_kernel(me_ref, gathered, mod, weight, own, own_old, sib, sib_old, hidden):
    _, _, c = place(me_ref)
    shift_row = mod[0:1, :]
    scale_row = 1.0 + mod[1:2, :]
    for out, head in ((sib_old, 1 - c), (own_old, c)):
        for t in range(3):
            at = pl.multiple_of(3072 + 256 * t + 128 * head, 128)
            out[:, :, 128 * t : 128 * t + 128] = gathered[:, :, pl.ds(at, 128)]
    for half in range(2):
        for i in range(4 * half, 4 * half + 4):
            values = gathered[i, :, 0:3072].astype(jnp.float32)
            mean = jnp.mean(values, axis=-1, keepdims=True)
            centred = values - mean
            var = jnp.mean(centred * centred, axis=-1, keepdims=True)
            normed = centred * lax.rsqrt(var + 1e-06)
            hidden[64 * i : 64 * i + 64, :] = (normed * scale_row + shift_row).astype(jnp.bfloat16)
        for pair in range(3):
            both = jnp.concatenate([weight[2 * pair], weight[2 * pair + 1]], axis=-1)
            result = jnp.dot(
                hidden[256 * half : 256 * half + 256, :], both, preferred_element_type=jnp.float32
            ).astype(jnp.bfloat16)
            for n in range(2):
                at = 2 * pair + n
                target = sib if at < 3 else own
                target[4 * half : 4 * half + 4, :, 128 * (at % 3) : 128 * (at % 3) + 128] = result[
                    :, 128 * n : 128 * n + 128
                ].reshape(4, 64, HD)


def project_qkv(me, gathered, mod, weight):
    shape = jax.ShapeDtypeStruct((8, 64, 3 * HD), jnp.bfloat16)
    return pl.pallas_call(
        qkv_kernel,
        out_shape=(shape,) * 4,
        in_specs=[SCALAR, NEAR, NEAR, NEAR],
        out_specs=(NEAR,) * 4,
        scratch_shapes=[pltpu.VMEM((512, 3072), jnp.bfloat16)],
        compiler_params=params(24),
        cost_estimate=cost(0.01),
    )(me, gathered, mod, weight)


def attend_kernel(me_ref, hide, own, own_old, sib, sib_old, out, query, keys, values, staged, out_sems):
    _, _, c = place(me_ref)
    for i, (new, old) in enumerate(((own, own_old), (sib, sib_old))):
        fresh = slice(512 * i, 512 * i + 512)
        query[fresh, :] = new[:, :, 0:128].reshape(512, HD)
        keys[fresh, :] = new[:, :, 128:256].reshape(512, HD)
        values[fresh, 0:128] = new[:, :, 256:384].reshape(512, HD)
        for k in range(8):
            at = 1024 + 96 * (8 * i + k)
            keys[at : at + 64, :] = old[k, :, 0:128]
            keys[at + 64 : at + 96, :] = old[k, 0:32, 128:256]
            values[at : at + 32, 0:128] = old[k, 32:64, 128:256]
            values[at + 32 : at + 96, 0:128] = old[k, :, 256:384]
    values[:, 128:256] = jnp.ones((2560, 128), jnp.bfloat16)
    scale = HD ** (-0.5) * math.log2(math.e)
    stores = []
    for i in range(8):
        scores = lax.dot_general(
            query[128 * i : 128 * i + 128, :],
            keys[...],
            (((1,), (1,)), ((), ())),
            preferred_element_type=jnp.float32,
        )
        fresh = scores[:, :1024]
        old = scores[:, 1024:] + hide[...]
        top = jnp.maximum(
            jnp.max(fresh, axis=-1, keepdims=True), jnp.max(old, axis=-1, keepdims=True)
        )
        weights = jnp.concatenate(
            [
                jnp.exp2((fresh - top) * scale).astype(jnp.bfloat16),
                jnp.exp2((old - top) * scale).astype(jnp.bfloat16),
            ],
            axis=-1,
        )
        summed = jnp.dot(weights, values[...], preferred_element_type=jnp.float32)
        result = (summed[:, :128] * (1.0 / summed[:, 128:])).astype(jnp.bfloat16)
        for n in range(2):
            dc, owner, y = i // 4, i % 4, n
            for to in range(NX):
                staged[to, y * 2 + (c ^ dc), (owner - to) % NX] = result[64 * n : 64 * n + 64]
        if owner == NX - 1:
            for y in range(NY):
                group = y * 2 + (c ^ dc)
                stores.append(
                    pltpu.make_async_copy(staged.at[:, group], out.at[:, group], out_sems.at[2 * dc + y])
                )
                stores[-1].start()
    for store in stores:
        store.wait()


def attend(me, hide, own, own_old, sib, sib_old):
    return pl.pallas_call(
        attend_kernel,
        out_shape=jax.ShapeDtypeStruct((NX, 4, NX, 64, HD), jnp.bfloat16),
        in_specs=[SCALAR] + [NEAR] * 5,
        out_specs=FAR,
        scratch_shapes=[
            pltpu.VMEM((1024, HD), jnp.bfloat16),
            pltpu.VMEM((2560, HD), jnp.bfloat16),
            pltpu.VMEM((2560, 2 * HD), jnp.bfloat16),
            pltpu.VMEM((NX, 4, NX, 64, HD), jnp.bfloat16),
            pltpu.SemaphoreType.DMA((NX,)),
        ],
        compiler_params=params(32),
        cost_estimate=cost(0.01),
    )(me, hide, own, own_old, sib, sib_old)


def collect_kernel(me_ref, w_own, w_c, w_y, w_yc, weight, sems):
    x, y, c = place(me_ref)
    copies = []
    for i, (ref, dy, dc) in enumerate(((w_own, 0, 0), (w_c, 0, 1), (w_y, 1, 0), (w_yc, 1, 1))):
        at = pl.multiple_of(((y ^ dy) * 2 + (c ^ dc)) * 192, 64)
        copies.append(pltpu.make_async_copy(ref, weight.at[pl.ds(at, 192), :], sems.at[i]))
        copies[-1].start()
    for copy in copies:
        copy.wait()


def collect(me, weights):
    return pl.pallas_call(
        collect_kernel,
        out_shape=jax.ShapeDtypeStruct((768, 2048), jnp.bfloat16),
        in_specs=[SCALAR] + [FAR] * 4,
        out_specs=NEAR,
        scratch_shapes=[pltpu.SemaphoreType.DMA((4,))],
        compiler_params=params(4),
        cost_estimate=cost(0.01),
    )(me, *weights)


def out_kernel(me_ref, heads, weight, gate, gathered, o0, o1, o2, o3, rows, kept, row_sems, kept_sems):
    x, y, _ = place(me_ref)
    columns = pl.ds(pl.multiple_of(x * 768, 768), 768)
    loads = [
        pltpu.make_async_copy(
            gathered.at[((x + i) & 3) * 2 + y, :, columns], kept.at[i], kept_sems.at[i]
        )
        for i in range(NX)
    ]
    parts = [
        pltpu.make_async_copy(heads.at[4 * i : 4 * i + 4], rows.at[4 * i : 4 * i + 4], row_sems.at[i])
        for i in range(4)
    ]
    for load in parts + loads:
        load.start()
    attn = jnp.zeros((256, 768), jnp.float32)
    for i in range(4):
        parts[i].wait()
        attn += lax.dot_general(
            jnp.concatenate([rows[j] for j in range(4 * i, 4 * i + 4)], axis=-1),
            weight[:, 512 * i : 512 * i + 512],
            (((1,), (1,)), ((), ())),
            preferred_element_type=jnp.float32,
        )
    attn = attn.astype(jnp.bfloat16).astype(jnp.float32)
    for i, out in enumerate((o0, o1, o2, o3)):
        loads[i].wait()
        values = kept[i].astype(jnp.float32)
        out[...] = (values + gate[...] * attn[64 * i : 64 * i + 64, :]).astype(jnp.bfloat16)


def project_out(me, heads, weight, gate, gathered):
    shape = jax.ShapeDtypeStruct((64, 768), jnp.bfloat16)
    return pl.pallas_call(
        out_kernel,
        out_shape=(shape,) * 4,
        in_specs=[SCALAR, FAR, NEAR, NEAR, FAR],
        out_specs=(NEAR,) * 4,
        scratch_shapes=[
            pltpu.VMEM((16, 256, HD), jnp.bfloat16),
            pltpu.VMEM((NX, 64, 768), jnp.bfloat16),
            pltpu.SemaphoreType.DMA((4,)),
            pltpu.SemaphoreType.DMA((NX,)),
        ],
        compiler_params=params(16),
        cost_estimate=cost(2),
    )(me, heads, weight, gate, gathered)


def join_kernel(me_ref, p0, p1, p2, p3, out, sems):
    x, _, _ = place(me_ref)
    copies = []
    for i, ref in enumerate((p0, p1, p2, p3)):
        columns = pl.ds(pl.multiple_of(((x + NX - i) & 3) * 768, 768), 768)
        copies.append(pltpu.make_async_copy(ref, out.at[:, columns], sems.at[i]))
        copies[-1].start()
    for copy in copies:
        copy.wait()


def join(me, pieces):
    return pl.pallas_call(
        join_kernel,
        out_shape=jax.ShapeDtypeStruct((64, 3072), jnp.bfloat16),
        in_specs=[SCALAR] + [NEAR] * 4,
        out_specs=FAR,
        scratch_shapes=[pltpu.SemaphoreType.DMA((4,))],
        compiler_params=params(32),
        cost_estimate=cost(0.01),
    )(me, *pieces)


def on_device(activations, modulation, w_qkv, w_out, stale_kv, section_micro, patch_micro):
    rows = activations[0]
    mod = modulation[0]
    index = lax.axis_index("seq").astype(jnp.int32)
    me = index.reshape(1)
    w_own = jnp.transpose(w_qkv[0], (1, 0, 2))
    out_own = jnp.transpose(w_out[0], (1, 0))
    owners = patch_micro.reshape(8, 2, 96).transpose(1, 0, 2)
    owners = jnp.where(index % 2 == 0, owners, owners[::-1]).reshape(1, -1)
    hide = jnp.where(owners != section_micro[0], 0.0, -jnp.inf).astype(jnp.float32)

    sent = pack(rows, stale_kv[0].reshape(192, 2048))
    gathered = lax.all_to_all(sent, "seq", 0, 0, tiled=True, axis_index_groups=LANES)
    w_sib = shift(w_own, dc=1)
    out_c = shift(out_own, dc=1)
    (out_late,) = following(gathered, out_own)
    out_y = shift(out_late, dy=1)
    out_yc = shift(out_y, dc=1)
    own, own_old, sib, sib_old = project_qkv(me, gathered, mod, collect_weights(w_own, w_sib))
    sib = shift(sib, dc=1)
    sib_old = shift(sib_old, dc=1)
    heads = attend(me, hide, own, own_old, sib, sib_old)
    (heads,) = following(out_y, heads)
    heads = lax.all_to_all(heads.reshape(16, 256, HD), "seq", 0, 0, tiled=True)
    weight = collect(me, (out_own, out_c, out_y, out_yc))
    gate = lax.dynamic_slice(mod, (2, index // (NY * NC) * 768), (1, 768))
    pieces = project_out(me, heads, weight, gate, gathered)
    arrived = {dx: hand_on(pieces[dx], dx) for dx in (2, 1, 3, 0)}
    return join(me, [arrived[dx] for dx in range(NX)])[None]


def solution(mesh):
    return jax.shard_map(
        on_device,
        mesh=mesh,
        in_specs=(
            P("pipe", "seq", None),
            P("pipe", None, None),
            P("pipe", None, None, "seq"),
            P("pipe", None, "seq"),
            P("pipe", None, "seq", None),
            P("pipe"),
            P(),
        ),
        out_specs=P("pipe", "seq", None),
        check_vma=False,
    )
```

```python
import math

import jax
import jax.numpy as jnp
from jax import lax
from jax.experimental import pallas as pl
from jax.experimental.pallas import tpu as pltpu
from jax.sharding import PartitionSpec as P

HD = 128
NX, NY, NC = 4, 2, 2
MIB = 1024 * 1024
SCALAR = pl.BlockSpec(memory_space=pltpu.SMEM)
FAR = pl.BlockSpec(memory_space=pltpu.HBM)
NEAR = pl.BlockSpec(memory_space=pltpu.VMEM)


def seq_index(x, y, core):
    return (x % NX) * NY * NC + (y % NY) * NC + core % NC


LANES = [[seq_index(x, y, c) for x in range(NX) for y in range(NY)] for c in range(NC)]


def shift(value, dx=0, dy=0, dc=0):
    pairs = [
        (seq_index(x, y, c), seq_index(x + dx, y + dy, c + dc))
        for x in range(NX)
        for y in range(NY)
        for c in range(NC)
    ]
    return lax.ppermute(value, "seq", pairs)


def hand_on(value, dx):
    count = lax.axis_size("pipe")
    pairs = [
        (s * 16 + seq_index(x, y, c), ((s + 1) % count) * 16 + seq_index(x + dx, y, c))
        for s in range(count)
        for x in range(NX)
        for y in range(NY)
        for c in range(NC)
    ]
    return lax.ppermute(value, ("pipe", "seq"), pairs)


def following(first, *values):
    return lax.optimization_barrier((first, *values))[1:]


def cost(microseconds):
    return pl.CostEstimate(flops=int(microseconds * 1e9), bytes_accessed=1, transcendentals=0)


def params(mib):
    return pltpu.CompilerParams(vmem_limit_bytes=mib * MIB)


def place(me_ref):
    me = me_ref[0]
    return me >> 2, (me >> 1) & 1, me & 1


def pack_kernel(rows, stale, out, held, old, load_sems, row_sems, stale_sems):
    loads = [
        pltpu.make_async_copy(rows, held, load_sems.at[0]),
        pltpu.make_async_copy(stale, old, load_sems.at[1]),
    ]
    for load in loads:
        load.start()
    copies = []
    loads[0].wait()
    for to in range(8):
        copies.append(pltpu.make_async_copy(held, out.at[to, :, 0:3072], row_sems.at[to]))
        copies[-1].start()
    loads[1].wait()
    for to in range(8):
        for t in range(3):
            copies.append(
                pltpu.make_async_copy(
                    old.at[64 * t : 64 * t + 64, 256 * to : 256 * to + 256],
                    out.at[to, :, 3072 + 256 * t : 3328 + 256 * t],
                    stale_sems.at[3 * to + t],
                )
            )
            copies[-1].start()
    for copy in copies:
        copy.wait()


def pack(rows, stale):
    return pl.pallas_call(
        pack_kernel,
        out_shape=jax.ShapeDtypeStruct((8, 64, 3840), jnp.bfloat16),
        in_specs=[FAR, FAR],
        out_specs=FAR,
        scratch_shapes=[
            pltpu.VMEM((64, 3072), jnp.bfloat16),
            pltpu.VMEM((192, 2048), jnp.bfloat16),
            pltpu.SemaphoreType.DMA((2,)),
            pltpu.SemaphoreType.DMA((8,)),
            pltpu.SemaphoreType.DMA((24,)),
        ],
        compiler_params=params(60),
        cost_estimate=cost(3),
    )(rows, stale)


def weights_kernel(w_own, w_sib, weight, sems):
    copies = []
    for i, ref in enumerate((w_sib, w_own)):
        copies.append(pltpu.make_async_copy(ref, weight.at[pl.ds(3 * i, 3)], sems.at[i]))
        copies[-1].start()
    for copy in copies:
        copy.wait()


def collect_weights(w_own, w_sib):
    return pl.pallas_call(
        weights_kernel,
        out_shape=jax.ShapeDtypeStruct((6, 3072, HD), jnp.bfloat16),
        in_specs=[FAR, FAR],
        out_specs=NEAR,
        scratch_shapes=[pltpu.SemaphoreType.DMA((2,))],
        compiler_params=params(16),
        cost_estimate=cost(0.01),
    )(w_own, w_sib)


def qkv_kernel(me_ref, gathered, mod, weight, own, own_old, sib, sib_old, hidden):
    _, _, c = place(me_ref)
    shift_row = mod[0:1, :]
    scale_row = 1.0 + mod[1:2, :]
    for out, head in ((sib_old, 1 - c), (own_old, c)):
        for t in range(3):
            at = pl.multiple_of(3072 + 256 * t + 128 * head, 128)
            out[:, :, 128 * t : 128 * t + 128] = gathered[:, :, pl.ds(at, 128)]
    for half in range(2):
        for i in range(4 * half, 4 * half + 4):
            values = gathered[i, :, 0:3072].astype(jnp.float32)
            mean = jnp.mean(values, axis=-1, keepdims=True)
            centred = values - mean
            var = jnp.mean(centred * centred, axis=-1, keepdims=True)
            normed = centred * lax.rsqrt(var + 1e-06)
            hidden[64 * i : 64 * i + 64, :] = (normed * scale_row + shift_row).astype(jnp.bfloat16)
        for pair in range(3):
            both = jnp.concatenate([weight[2 * pair], weight[2 * pair + 1]], axis=-1)
            result = jnp.dot(
                hidden[256 * half : 256 * half + 256, :], both, preferred_element_type=jnp.float32
            ).astype(jnp.bfloat16)
            for n in range(2):
                at = 2 * pair + n
                target = sib if at < 3 else own
                target[4 * half : 4 * half + 4, :, 128 * (at % 3) : 128 * (at % 3) + 128] = result[
                    :, 128 * n : 128 * n + 128
                ].reshape(4, 64, HD)


def project_qkv(me, gathered, mod, weight):
    shape = jax.ShapeDtypeStruct((8, 64, 3 * HD), jnp.bfloat16)
    return pl.pallas_call(
        qkv_kernel,
        out_shape=(shape,) * 4,
        in_specs=[SCALAR, NEAR, NEAR, NEAR],
        out_specs=(NEAR,) * 4,
        scratch_shapes=[pltpu.VMEM((512, 3072), jnp.bfloat16)],
        compiler_params=params(24),
        cost_estimate=cost(0.01),
    )(me, gathered, mod, weight)


def attend_kernel(
    me_ref, hide, own, own_old, sib, sib_far, out, query, keys, values, staged, sib_old, load_sem, out_sems
):
    _, _, c = place(me_ref)
    load = pltpu.make_async_copy(sib_far, sib_old, load_sem.at[0])
    load.start()
    for i, (new, old) in enumerate(((own, own_old), (sib, sib_old))):
        fresh = slice(512 * i, 512 * i + 512)
        query[fresh, :] = new[:, :, 0:128].reshape(512, HD)
        keys[fresh, :] = new[:, :, 128:256].reshape(512, HD)
        values[fresh, 0:128] = new[:, :, 256:384].reshape(512, HD)
        if i == 1:
            load.wait()
        for k in range(8):
            at = 1024 + 96 * (8 * i + k)
            keys[at : at + 64, :] = old[k, :, 0:128]
            keys[at + 64 : at + 96, :] = old[k, 0:32, 128:256]
            values[at : at + 32, 0:128] = old[k, 32:64, 128:256]
            values[at + 32 : at + 96, 0:128] = old[k, :, 256:384]
    values[:, 128:256] = jnp.ones((2560, 128), jnp.bfloat16)
    scale = HD ** (-0.5) * math.log2(math.e)
    stores = []
    for i in range(8):
        scores = lax.dot_general(
            query[128 * i : 128 * i + 128, :],
            keys[...],
            (((1,), (1,)), ((), ())),
            preferred_element_type=jnp.float32,
        )
        fresh = scores[:, :1024]
        old = scores[:, 1024:] + hide[...]
        top = jnp.maximum(
            jnp.max(fresh, axis=-1, keepdims=True), jnp.max(old, axis=-1, keepdims=True)
        )
        weights = jnp.concatenate(
            [
                jnp.exp2((fresh - top) * scale).astype(jnp.bfloat16),
                jnp.exp2((old - top) * scale).astype(jnp.bfloat16),
            ],
            axis=-1,
        )
        summed = jnp.dot(weights, values[...], preferred_element_type=jnp.float32)
        result = (summed[:, :128] * (1.0 / summed[:, 128:])).astype(jnp.bfloat16)
        for n in range(2):
            dc, owner, y = i // 4, i % 4, n
            for to in range(NX):
                staged[to, y * 2 + (c ^ dc), (owner - to) % NX] = result[64 * n : 64 * n + 64]
        if owner == NX - 1:
            for y in range(NY):
                group = y * 2 + (c ^ dc)
                stores.append(
                    pltpu.make_async_copy(staged.at[:, group], out.at[:, group], out_sems.at[2 * dc + y])
                )
                stores[-1].start()
    for store in stores:
        store.wait()


def attend(me, hide, own, own_old, sib, sib_old):
    return pl.pallas_call(
        attend_kernel,
        out_shape=jax.ShapeDtypeStruct((NX, 4, NX, 64, HD), jnp.bfloat16),
        in_specs=[SCALAR] + [NEAR] * 4 + [FAR],
        out_specs=FAR,
        scratch_shapes=[
            pltpu.VMEM((1024, HD), jnp.bfloat16),
            pltpu.VMEM((2560, HD), jnp.bfloat16),
            pltpu.VMEM((2560, 2 * HD), jnp.bfloat16),
            pltpu.VMEM((NX, 4, NX, 64, HD), jnp.bfloat16),
            pltpu.VMEM((8, 64, 3 * HD), jnp.bfloat16),
            pltpu.SemaphoreType.DMA((1,)),
            pltpu.SemaphoreType.DMA((NX,)),
        ],
        compiler_params=params(32),
        cost_estimate=cost(0.01),
    )(me, hide, own, own_old, sib, sib_old)


def collect_kernel(me_ref, w_own, w_c, w_y, w_yc, weight, sems):
    x, y, c = place(me_ref)
    copies = []
    for i, (ref, dy, dc) in enumerate(((w_own, 0, 0), (w_c, 0, 1), (w_y, 1, 0), (w_yc, 1, 1))):
        at = pl.multiple_of(((y ^ dy) * 2 + (c ^ dc)) * 192, 64)
        copies.append(pltpu.make_async_copy(ref, weight.at[pl.ds(at, 192), :], sems.at[i]))
        copies[-1].start()
    for copy in copies:
        copy.wait()


def collect(me, weights):
    return pl.pallas_call(
        collect_kernel,
        out_shape=jax.ShapeDtypeStruct((768, 2048), jnp.bfloat16),
        in_specs=[SCALAR] + [FAR] * 4,
        out_specs=NEAR,
        scratch_shapes=[pltpu.SemaphoreType.DMA((4,))],
        compiler_params=params(4),
        cost_estimate=cost(0.01),
    )(me, *weights)


def out_kernel(me_ref, heads, weight, gate, gathered, o0, o1, o2, o3, rows, kept, row_sems, kept_sems):
    x, y, _ = place(me_ref)
    columns = pl.ds(pl.multiple_of(x * 768, 768), 768)
    loads = [
        pltpu.make_async_copy(
            gathered.at[((x + i) & 3) * 2 + y, :, columns], kept.at[i], kept_sems.at[i]
        )
        for i in range(NX)
    ]
    parts = [
        pltpu.make_async_copy(heads.at[4 * i : 4 * i + 4], rows.at[4 * i : 4 * i + 4], row_sems.at[i])
        for i in range(4)
    ]
    for load in parts + loads:
        load.start()
    attn = jnp.zeros((256, 768), jnp.float32)
    for i in range(4):
        parts[i].wait()
        attn += lax.dot_general(
            jnp.concatenate([rows[j] for j in range(4 * i, 4 * i + 4)], axis=-1),
            weight[:, 512 * i : 512 * i + 512],
            (((1,), (1,)), ((), ())),
            preferred_element_type=jnp.float32,
        )
    attn = attn.astype(jnp.bfloat16).astype(jnp.float32)
    for i, out in enumerate((o0, o1, o2, o3)):
        loads[i].wait()
        values = kept[i].astype(jnp.float32)
        out[...] = (values + gate[...] * attn[64 * i : 64 * i + 64, :]).astype(jnp.bfloat16)


def project_out(me, heads, weight, gate, gathered):
    shape = jax.ShapeDtypeStruct((64, 768), jnp.bfloat16)
    return pl.pallas_call(
        out_kernel,
        out_shape=(shape,) * 4,
        in_specs=[SCALAR, FAR, NEAR, NEAR, FAR],
        out_specs=(NEAR,) * 4,
        scratch_shapes=[
            pltpu.VMEM((16, 256, HD), jnp.bfloat16),
            pltpu.VMEM((NX, 64, 768), jnp.bfloat16),
            pltpu.SemaphoreType.DMA((4,)),
            pltpu.SemaphoreType.DMA((NX,)),
        ],
        compiler_params=params(16),
        cost_estimate=cost(2),
    )(me, heads, weight, gate, gathered)


def join_kernel(me_ref, p0, p1, p2, p3, out, sems):
    x, _, _ = place(me_ref)
    copies = []
    for i, ref in enumerate((p0, p1, p2, p3)):
        columns = pl.ds(pl.multiple_of(((x + NX - i) & 3) * 768, 768), 768)
        copies.append(pltpu.make_async_copy(ref, out.at[:, columns], sems.at[i]))
        copies[-1].start()
    for copy in copies:
        copy.wait()


def join(me, pieces):
    return pl.pallas_call(
        join_kernel,
        out_shape=jax.ShapeDtypeStruct((64, 3072), jnp.bfloat16),
        in_specs=[SCALAR] + [NEAR] * 4,
        out_specs=FAR,
        scratch_shapes=[pltpu.SemaphoreType.DMA((4,))],
        compiler_params=params(32),
        cost_estimate=cost(0.01),
    )(me, *pieces)


def on_device(activations, modulation, w_qkv, w_out, stale_kv, section_micro, patch_micro):
    rows = activations[0]
    mod = modulation[0]
    index = lax.axis_index("seq").astype(jnp.int32)
    me = index.reshape(1)
    w_own = jnp.transpose(w_qkv[0], (1, 0, 2))
    out_own = jnp.transpose(w_out[0], (1, 0))
    owners = patch_micro.reshape(8, 2, 96).transpose(1, 0, 2)
    owners = jnp.where(index % 2 == 0, owners, owners[::-1]).reshape(1, -1)
    hide = jnp.where(owners != section_micro[0], 0.0, -jnp.inf).astype(jnp.float32)

    sent = pack(rows, stale_kv[0].reshape(192, 2048))
    gathered = lax.all_to_all(sent, "seq", 0, 0, tiled=True, axis_index_groups=LANES)
    w_sib = shift(w_own, dc=1)
    out_c = shift(out_own, dc=1)
    (out_late,) = following(gathered, out_own)
    out_y = shift(out_late, dy=1)
    out_yc = shift(out_y, dc=1)
    own, own_old, sib, sib_old = project_qkv(me, gathered, mod, collect_weights(w_own, w_sib))
    sib = shift(sib, dc=1)
    sib_old = shift(sib_old, dc=1)
    heads = attend(me, hide, own, own_old, sib, sib_old)
    (heads,) = following(out_y, heads)
    heads = lax.all_to_all(heads.reshape(16, 256, HD), "seq", 0, 0, tiled=True)
    weight = collect(me, (out_own, out_c, out_y, out_yc))
    gate = lax.dynamic_slice(mod, (2, index // (NY * NC) * 768), (1, 768))
    pieces = project_out(me, heads, weight, gate, gathered)
    arrived = {dx: hand_on(pieces[dx], dx) for dx in (2, 1, 3, 0)}
    return join(me, [arrived[dx] for dx in range(NX)])[None]


def solution(mesh):
    return jax.shard_map(
        on_device,
        mesh=mesh,
        in_specs=(
            P("pipe", "seq", None),
            P("pipe", None, None),
            P("pipe", None, None, "seq"),
            P("pipe", None, "seq"),
            P("pipe", None, "seq", None),
            P("pipe"),
            P(),
        ),
        out_specs=P("pipe", "seq", None),
        check_vma=False,
    )
```
